512 devices in a mesh: band: 16 (over y, z_lo), fft: 32 (over z_hi, x, core).
Axes of the slice: x: 4, y: 4, z: 16 (z_hi: 4, z_lo: 4; z = z_hi * 4 + z_lo), core: 2. Of those that a mesh axis runs over, the one named last changes fastest.
Arguments:
- orbitals: float32 [64, 128, 128, 128], P('band', 'fft'), may hold values from -6 to 6
- kernel: float32 [128, 128, 128], P(None, 'fft'), as said below
- owners: int32 [2], replicated, may hold values from 0 to 15, as said below
- picks: int32 [2, 1], replicated, may hold values from 0 to 3, as said below
Outputs:
- exchange_action: float32 [64, 128, 128, 128], P('band', 'fft')
The draws below stay inside these ranges and needn't reach their ends.
Inputs may be any that keep to these rules, and one draw needn't show every extreme that they name: kernel is positive and takes equal values at each frequency vector and at its negative, indices taken modulo 128. `owners`: the steps name different band groups. `picks`: all entries are different positions.
All inputs are finite; a program needn't handle non-finite values.
Results may differ from the reference program's by a relative error of at most 0.00016.
Values sent between devices are 32-bit elements; how exact they have to be, the bound alone decides.
No kernel may reach another device: no remote copies, remote signals or barrier semaphores. Data moves between devices by JAX's collectives and lax.ppermute only.
A program may use at most 64 MiB of HBM per device.

```python
import jax
import jax.numpy as jnp
from jax import lax

NG = 128
ORB_DEV = 4
BCAST = 1
STEPS = 2
NORB = 64
N_BAND = 16


def reach_top(values, top):
    present = jnp.any(values == top)
    forced = values.at[-1].set(top)
    return jnp.where(present, values, forced)


def draw_kernel(key, part):
    key = jax.random.fold_in(key, 11)
    count = NG
    freq = jnp.arange(count)
    folded = jnp.minimum(freq, count - freq).astype(jnp.float32)
    squared = folded[:, None, None] ** 2 + folded[None, :, None] ** 2 + folded[None, None, :] ** 2
    width = count / 10.0
    base = 10.0 / (1.0 + squared / (width * width))
    noise = jax.random.normal(key, (count, count, count), jnp.float32)
    mirror = -freq % count
    flipped = noise[mirror][:, mirror][:, :, mirror]
    factor = jnp.exp(0.25 * (noise + flipped))
    return (base * factor).astype(jnp.float32)


def draw_owners(key, part):
    key = jax.random.fold_in(key, 23)
    order = jax.random.permutation(key, N_BAND).astype(jnp.int32)
    return reach_top(order[:STEPS], N_BAND - 1).astype(jnp.int32)


def draw_picks(key, part):
    key = jax.random.fold_in(key, 37)
    order = jax.random.permutation(key, ORB_DEV).astype(jnp.int32)
    chosen = reach_top(order[:STEPS * BCAST], ORB_DEV - 1)
    return chosen.reshape((STEPS, BCAST)).astype(jnp.int32)


def shard_levels(own_key, extent, pieces, smallest, top_value):
    gain, own = 1.0, jax.random.fold_in(own_key, 6)
    for dim, parts in pieces:
        steps = jnp.exp(jax.random.uniform(jax.random.fold_in(own, dim), (parts,), jnp.float32, smallest / len(pieces), top_value / len(pieces)))
        gain = gain * jnp.repeat(steps, extent[dim] // parts).reshape([-1 if axis == dim else 1 for axis in range(len(extent))])
    return gain


def gaussian(rng, dims, spread, bound, split=(), held_as=jnp.bfloat16):
    loudness = shard_levels(rng, dims, split, -0.22, 0.18) if split else 1.0
    values = jax.random.normal(rng, dims, jnp.float32) * spread * loudness
    return jnp.minimum(jnp.maximum(values, -bound), bound).astype(held_as)


def setup_inputs(seed: int = 0) -> dict:
    splits = jax.random.split(jax.random.key(seed), 5)
    return {
        "orbitals": gaussian(splits[0], (NORB, NG, NG, NG), 1.0, 6.0, ((0, 16), (1, 32)), jnp.float32),
        "kernel": draw_kernel(jax.random.fold_in(splits[4], 71), 0),
        "owners": draw_owners(jax.random.fold_in(splits[4], 71), 0),
        "picks": draw_picks(jax.random.fold_in(splits[4], 71), 0),
    }


def reference(orbitals, kernel, owners, picks):
    total = jnp.zeros(orbitals.shape, jnp.float32)
    for step in range(STEPS):
        for slot in range(BCAST):
            index = (owners[step] * ORB_DEV + picks[step, slot]).astype(jnp.int32)
            sent = lax.dynamic_index_in_dim(orbitals, index, 0, keepdims=False)

            def single(orbital):
                density = orbital * sent
                spectrum = jnp.fft.fftn(density) * kernel
                potential = jnp.real(jnp.fft.ifftn(spectrum)).astype(jnp.float32)
                return -(sent * potential)

            total = total + lax.map(single, orbitals)
    return total
```

```python
import functools

import jax
import jax.numpy as jnp
import ml_dtypes
import numpy as np
from jax import lax
from jax.experimental import pallas as pl
from jax.experimental.pallas import tpu as pltpu
from jax.sharding import Mesh, PartitionSpec as P

NG = 128
SIDE = 4
GROUP = 32
SCALE = 1.0 / float(NG) ** 3


def split_table(matrix):
    high = matrix.astype(np.float32).astype(ml_dtypes.bfloat16)
    low = (matrix - high.astype(np.float64)).astype(ml_dtypes.bfloat16)
    return np.stack([high, low])


def real_form(rows, cols, sign):
    angle = 2.0 * np.pi * ((rows[:, None] * cols[None, :]) % NG) / NG
    cosine, sine = np.cos(angle), sign * np.sin(angle)
    return np.block([[cosine, -sine], [sine, cosine]])


def make_tables():
    plain = np.arange(NG)
    rank = np.arange(GROUP)
    y, x, core = rank // 8, rank // 2 % 4, rank % 2
    held = (np.arange(SIDE)[None, :] * 32 + (x * 8 + core * 4 + y)[:, None]).reshape(-1)
    mixed = (rank[:, None, None] * SIDE + np.arange(2)[None, :, None] * NG + np.arange(SIDE)[None, None, :]).reshape(-1)
    z_fwd = real_form(plain, plain, -1.0).T
    y_fwd = real_form(held, plain, -1.0)[mixed]
    x_fwd = real_form(plain, held, -1.0)
    x_inv = real_form(held, plain, 1.0)
    y_inv = real_form(plain, held, 1.0)[:, mixed]
    z_inv = real_form(plain, plain, 1.0).T
    return [split_table(t) for t in (z_fwd, y_fwd, x_fwd, x_inv, y_inv, z_inv)]


def split(values):
    high = values.astype(jnp.bfloat16)
    return high, (values - high.astype(jnp.float32)).astype(jnp.bfloat16)


def dot(a, b):
    return jnp.dot(a, b, preferred_element_type=jnp.float32)


def times(values, table):
    high, low = split(values)
    return dot(high, table[0]) + (dot(low, table[0]) + dot(high, table[1]))


def apply(table, values):
    high, low = split(values)
    return dot(table[0], high) + (dot(table[0], low) + dot(table[1], high))


def forward_kernel(psi_ref, sent_ref, z_ref, y_ref, out_ref):
    def per_plane(b, carry):
        base = pl.multiple_of(b * SIDE, SIDE)
        first = sent_ref[pl.ds(base, SIDE), 0].reshape(NG, NG)
        second = sent_ref[pl.ds(base, SIDE), 1].reshape(NG, NG)
        rows = []
        for a in range(SIDE):
            psi = psi_ref[base + a]
            rows.append(jnp.concatenate([psi * first, psi * second], axis=1))
        lines = times(jnp.concatenate(rows, axis=0), z_ref)
        cols = []
        for a in range(SIDE):
            part = lines[a * NG : (a + 1) * NG]
            cols.append(jnp.concatenate([part[:, :NG], part[:, NG:]], axis=0))
        spectrum = apply(y_ref, jnp.concatenate(cols, axis=1))
        for a in range(SIDE):
            out_ref[:, base + a] = spectrum[:, a * NG : (a + 1) * NG].reshape(GROUP, 8, NG)
        return carry

    lax.fori_loop(0, SIDE, per_plane, 0)


def middle_kernel(in_ref, kernel_ref, fwd_ref, inv_ref, out_ref):
    for ky in range(SIDE):
        cols = []
        for a in range(SIDE):
            at = a * 8 + ky
            cols.append(
                jnp.concatenate([in_ref[pl.ds(at, NG, stride=32), :], in_ref[pl.ds(at + 4, NG, stride=32), :]], axis=0)
            )
        spectrum = apply(fwd_ref, jnp.concatenate(cols, axis=1))
        weight = kernel_ref[ky]
        weight = jnp.concatenate([weight, weight], axis=0)
        weight = jnp.concatenate([weight] * SIDE, axis=1)
        back = apply(inv_ref, spectrum * weight)
        for a in range(SIDE):
            at = a * 8 + ky
            part = back[:, a * NG : (a + 1) * NG]
            out_ref[pl.ds(at, NG, stride=32), :] = part[:NG]
            out_ref[pl.ds(at + 4, NG, stride=32), :] = part[NG:]


def inverse_kernel(in_ref, sent_ref, y_ref, z_ref, out_ref):
    def per_plane(b, carry):
        base = pl.multiple_of(b * SIDE, SIDE)
        first = sent_ref[pl.ds(base, SIDE), 0].reshape(NG, NG)
        second = sent_ref[pl.ds(base, SIDE), 1].reshape(NG, NG)
        cols = [in_ref[:, base + a].reshape(2 * NG, NG) for a in range(SIDE)]
        lines = apply(y_ref, jnp.concatenate(cols, axis=1))
        rows = []
        for a in range(SIDE):
            part = lines[:, a * NG : (a + 1) * NG]
            rows.append(jnp.concatenate([part[:NG], part[NG:]], axis=1))
        field = times(jnp.concatenate(rows, axis=0), z_ref)
        for a in range(SIDE):
            part = field[a * NG : (a + 1) * NG]
            out_ref[base + a] = (first * part[:, :NG] + second * part[:, NG:]) * (-SCALE)
        return carry

    lax.fori_loop(0, SIDE, per_plane, 0)


def call(kernel, shape, flops, *args):
    moved = sum(int(np.prod(a.shape)) * a.dtype.itemsize for a in args) + 4 * int(np.prod(shape))
    return pl.pallas_call(
        kernel,
        out_shape=jax.ShapeDtypeStruct(shape, jnp.float32),
        compiler_params=pltpu.CompilerParams(vmem_limit_bytes=40 * 1024 * 1024),
        cost_estimate=pl.CostEstimate(flops=flops, bytes_accessed=moved, transcendentals=0),
    )(*args)


def body(tables, orbitals, kernel, owners, picks):
    z_fwd, y_fwd, x_fwd, x_inv, y_inv, z_inv = [jnp.asarray(t) for t in tables]
    steps = owners.shape[0]

    chosen = jnp.take(orbitals, picks[:, 0], axis=0).reshape(steps, SIDE, SIDE, 32, NG)
    chosen = jnp.transpose(chosen, (1, 2, 0, 3, 4)).reshape(SIDE * SIDE, steps, 32, NG)
    offered = lax.all_to_all(chosen, ("y", "zl"), 0, 0, tiled=True)
    piece = jnp.stack([lax.dynamic_index_in_dim(offered, owners[s], 0, keepdims=False)[s] for s in range(steps)])

    orbitals, piece = lax.optimization_barrier((orbitals.reshape(SIDE * SIDE, NG, NG), piece))
    sent = lax.all_gather(piece, ("zh", "zl"), axis=0, tiled=False)
    psi = lax.all_to_all(orbitals, ("zh", "y"), 0, 0, tiled=True)

    own = lax.dynamic_index_in_dim(kernel, lax.axis_index("y"), 1, keepdims=False)
    own, psi = lax.optimization_barrier((own, psi))
    weight = lax.all_gather(own, "zh", axis=0, tiled=False)

    work = 2 * 2 * 3 * 2048 * 256 * 256
    group = ("y", "x", "c")
    spectrum = call(forward_kernel, (GROUP, 16, 8, NG), work, psi, sent, z_fwd, y_fwd)
    spectrum = lax.all_to_all(spectrum, group, 0, 0, tiled=True).reshape(GROUP * NG, NG)
    spectrum = call(middle_kernel, (GROUP * NG, NG), work, spectrum, weight, x_fwd, x_inv)
    spectrum = lax.all_to_all(spectrum.reshape(GROUP, 16, 8, NG), group, 0, 0, tiled=True)
    action = call(inverse_kernel, (16, NG, NG), work, spectrum, sent, y_inv, z_inv)
    action = lax.all_to_all(action, ("zh", "y"), 0, 0, tiled=True)
    return action.reshape(SIDE, SIDE, NG, NG)


def solution(mesh):
    fine = Mesh(np.asarray(mesh.devices).reshape(4, 4, 4, 4, 2), ("y", "zl", "zh", "x", "c"))
    band, fft = ("y", "zl"), ("zh", "x", "c")
    placed = (P(band, fft, None, None), P(None, fft, None), P(), P())
    return jax.shard_map(
        functools.partial(body, make_tables()),
        mesh=fine,
        in_specs=placed,
        out_specs=P(band, fft, None, None),
        check_vma=False,
    )
```

```python
import functools

import jax
import jax.numpy as jnp
import ml_dtypes
import numpy as np
from jax import lax
from jax.experimental import pallas as pl
from jax.experimental.pallas import tpu as pltpu
from jax.sharding import Mesh, PartitionSpec as P

NG = 128
SIDE = 4
GROUP = 32
SCALE = 1.0 / float(NG) ** 3


def split_table(matrix):
    high = matrix.astype(np.float32).astype(ml_dtypes.bfloat16)
    low = (matrix - high.astype(np.float64)).astype(ml_dtypes.bfloat16)
    return np.stack([high, low])


def real_form(rows, cols, sign):
    angle = 2.0 * np.pi * ((rows[:, None] * cols[None, :]) % NG) / NG
    cosine, sine = np.cos(angle), sign * np.sin(angle)
    return np.block([[cosine, -sine], [sine, cosine]])


def make_tables():
    plain = np.arange(NG)
    rank = np.arange(GROUP)
    y, x, core = rank // 8, rank // 2 % 4, rank % 2
    held = (np.arange(SIDE)[None, :] * 32 + (x * 8 + core * 4 + y)[:, None]).reshape(-1)
    mixed = (rank[:, None, None] * SIDE + np.arange(2)[None, :, None] * NG + np.arange(SIDE)[None, None, :]).reshape(-1)
    z_fwd = real_form(plain, plain, -1.0).T
    y_fwd = real_form(held, plain, -1.0)[mixed]
    x_fwd = real_form(plain, held, -1.0)
    x_inv = real_form(held, plain, 1.0)
    y_inv = real_form(plain, held, 1.0)[:, mixed]
    z_inv = real_form(plain, plain, 1.0).T
    return [split_table(t) for t in (z_fwd, y_fwd, x_fwd, x_inv, y_inv, z_inv)]


def split(values):
    high = values.astype(jnp.bfloat16)
    return high, (values - high.astype(jnp.float32)).astype(jnp.bfloat16)


def dot(a, b):
    return jnp.dot(a, b, preferred_element_type=jnp.float32)


def times(values, table):
    high, low = split(values)
    return dot(high, table[0]) + (dot(low, table[0]) + dot(high, table[1]))


def apply(table, values):
    high, low = split(values)
    return dot(table[0], high) + (dot(table[0], low) + dot(table[1], high))


def plane(sent_ref, place_ref, b, s):
    return jnp.concatenate([sent_ref[place_ref[b * SIDE + q], s] for q in range(SIDE)], axis=0)


def forward_kernel(place_ref, psi_ref, sent_ref, z_ref, y_ref, out_ref):
    for b in range(SIDE):
        first, second = plane(sent_ref, place_ref, b, 0), plane(sent_ref, place_ref, b, 1)
        rows = []
        for a in range(SIDE):
            psi = psi_ref[b * SIDE + a]
            rows.append(jnp.concatenate([psi * first, psi * second], axis=1))
        lines = times(jnp.concatenate(rows, axis=0), z_ref)
        cols = []
        for a in range(SIDE):
            part = lines[a * NG : (a + 1) * NG]
            cols.append(jnp.concatenate([part[:, :NG], part[:, NG:]], axis=0))
        spectrum = apply(y_ref, jnp.concatenate(cols, axis=1))
        for a in range(SIDE):
            out_ref[:, b * SIDE + a] = spectrum[:, a * NG : (a + 1) * NG].reshape(GROUP, 8, NG)


def middle_kernel(place_ref, in_ref, kernel_ref, fwd_ref, inv_ref, out_ref):
    for ky in range(SIDE):
        cols = []
        for a in range(SIDE):
            at = a * 8 + ky
            cols.append(
                jnp.concatenate([in_ref[pl.ds(at, NG, stride=32), :], in_ref[pl.ds(at + 4, NG, stride=32), :]], axis=0)
            )
        spectrum = apply(fwd_ref, jnp.concatenate(cols, axis=1))
        weight = kernel_ref[place_ref[16 + ky]]
        weight = jnp.concatenate([weight, weight], axis=0)
        weight = jnp.concatenate([weight] * SIDE, axis=1)
        back = apply(inv_ref, spectrum * weight)
        for a in range(SIDE):
            at = a * 8 + ky
            part = back[:, a * NG : (a + 1) * NG]
            out_ref[pl.ds(at, NG, stride=32), :] = part[:NG]
            out_ref[pl.ds(at + 4, NG, stride=32), :] = part[NG:]


def inverse_kernel(place_ref, in_ref, sent_ref, y_ref, z_ref, out_ref):
    for b in range(SIDE):
        first, second = plane(sent_ref, place_ref, b, 0), plane(sent_ref, place_ref, b, 1)
        cols = [in_ref[:, b * SIDE + a].reshape(2 * NG, NG) for a in range(SIDE)]
        lines = apply(y_ref, jnp.concatenate(cols, axis=1))
        rows = []
        for a in range(SIDE):
            part = lines[:, a * NG : (a + 1) * NG]
            rows.append(jnp.concatenate([part[:NG], part[NG:]], axis=1))
        field = times(jnp.concatenate(rows, axis=0), z_ref)
        for a in range(SIDE):
            part = field[a * NG : (a + 1) * NG]
            out_ref[b * SIDE + a] = (first * part[:, :NG] + second * part[:, NG:]) * (-SCALE)


WORK = 2 * 2 * 3 * 2048 * 256 * 256


def call(kernel, shapes, place, *args):
    moved = sum(int(np.prod(a.shape)) * a.dtype.itemsize for a in args)
    moved += 4 * sum(int(np.prod(shape)) for shape in shapes)
    shapes = [jax.ShapeDtypeStruct(shape, jnp.float32) for shape in shapes]
    whole = pl.BlockSpec(memory_space=pltpu.VMEM)
    return pl.pallas_call(
        kernel,
        out_shape=shapes,
        in_specs=[pl.BlockSpec(memory_space=pltpu.SMEM)] + [whole] * len(args),
        out_specs=[whole] * len(shapes),
        compiler_params=pltpu.CompilerParams(vmem_limit_bytes=40 * 1024 * 1024),
        cost_estimate=pl.CostEstimate(flops=WORK, bytes_accessed=moved, transcendentals=0),
    )(place, *args)


def shift(values, axes, count, by):
    return lax.ppermute(values, axes, [(i, (i + by) % count) for i in range(count)])


def body(tables, orbitals, kernel, owners, picks):
    z_fwd, y_fwd, x_fwd, x_inv, y_inv, z_inv = [jnp.asarray(t) for t in tables]
    steps = owners.shape[0]
    y, zh, zl = lax.axis_index("y"), lax.axis_index("zh"), lax.axis_index("zl")

    psi = lax.all_to_all(orbitals.reshape(SIDE * SIDE, NG, NG), ("zh", "y"), 0, 0, tiled=True)

    def select(found, distance):
        return jnp.stack([lax.select_n(distance[s], *[f[s] for f in found]) for s in range(steps)])

    found = []
    for k in range(SIDE):
        at = (y + k) % SIDE
        part = [lax.dynamic_slice(orbitals, (picks[s, 0], at, 0, 0), (1, 1, NG, NG))[0, 0] for s in range(steps)]
        found.append(jnp.stack(part) if k == 0 else shift(jnp.stack(part), "y", SIDE, k))
    chosen = select(found, (y - owners // SIDE) % SIDE).reshape(steps, SIDE, 32, NG)
    found = []
    for k in range(SIDE):
        part = lax.dynamic_index_in_dim(chosen, (zl + k) % SIDE, 1, keepdims=False)
        found.append(part if k == 0 else shift(part, "zl", SIDE, k))
    sent = select(found, (zl - owners % SIDE) % SIDE)
    sent, psi = lax.optimization_barrier((sent, psi))
    sent = lax.all_to_all(jnp.broadcast_to(sent, (SIDE,) + sent.shape), "zh", 0, 0, tiled=True)
    sent = lax.all_to_all(jnp.broadcast_to(sent, (SIDE,) + sent.shape), "zl", 0, 0, tiled=True)
    sent = sent.reshape(16, steps, 32, NG)
    place = jnp.arange(16, dtype=jnp.int32)
    quarter = place % SIDE * SIDE + place // SIDE
    place = jnp.concatenate([quarter, jnp.arange(SIDE, dtype=jnp.int32)])

    own = lax.dynamic_index_in_dim(kernel, y, 1, keepdims=False)
    own, psi, sent = lax.optimization_barrier((own, psi, sent))
    weight = lax.all_gather(own, "zh", axis=0, tiled=False)

    group = ("y", "x", "c")
    (spectrum,) = call(forward_kernel, [(GROUP, 16, 8, NG)], place, psi, sent, z_fwd, y_fwd)
    spectrum = lax.all_to_all(spectrum, group, 0, 0, tiled=True).reshape(GROUP * NG, NG)
    (spectrum,) = call(middle_kernel, [(GROUP * NG, NG)], place, spectrum, weight, x_fwd, x_inv)
    spectrum = lax.all_to_all(spectrum.reshape(GROUP, 16, 8, NG), group, 0, 0, tiled=True)
    (action,) = call(inverse_kernel, [(16, NG, NG)], place, spectrum, sent, y_inv, z_inv)
    action = lax.all_to_all(action, ("zh", "y"), 0, 0, tiled=True)
    return action.reshape(SIDE, SIDE, NG, NG)


def solution(mesh):
    fine = Mesh(np.asarray(mesh.devices).reshape(4, 4, 4, 4, 2), ("y", "zl", "zh", "x", "c"))
    band, fft = ("y", "zl"), ("zh", "x", "c")
    placed = (P(band, fft, None, None), P(None, fft, None), P(), P())
    return jax.shard_map(
        functools.partial(body, make_tables()),
        mesh=fine,
        in_specs=placed,
        out_specs=P(band, fft, None, None),
        check_vma=False,
    )
```

```python
import functools

import jax
import jax.numpy as jnp
import ml_dtypes
import numpy as np
from jax import lax
from jax.experimental import pallas as pl
from jax.experimental.pallas import tpu as pltpu
from jax.sharding import Mesh, PartitionSpec as P

NG = 128
SIDE = 4
GROUP = 32
SCALE = 1.0 / float(NG) ** 3


def split_table(matrix):
    high = matrix.astype(np.float32).astype(ml_dtypes.bfloat16)
    low = (matrix - high.astype(np.float64)).astype(ml_dtypes.bfloat16)
    return np.stack([high, low])


def real_form(rows, cols, sign):
    angle = 2.0 * np.pi * ((rows[:, None] * cols[None, :]) % NG) / NG
    cosine, sine = np.cos(angle), sign * np.sin(angle)
    return np.block([[cosine, -sine], [sine, cosine]])


def make_tables():
    plain = np.arange(NG)
    rank = np.arange(GROUP)
    y, x, core = rank // 8, rank // 2 % 4, rank % 2
    held = (np.arange(SIDE)[None, :] * 32 + (x * 8 + core * 4 + y)[:, None]).reshape(-1)
    mixed = (rank[:, None, None] * SIDE + np.arange(2)[None, :, None] * NG + np.arange(SIDE)[None, None, :]).reshape(-1)
    z_fwd = real_form(plain, plain, -1.0).T
    y_fwd = real_form(held, plain, -1.0)[mixed]
    x_fwd = real_form(plain, held, -1.0)
    x_inv = real_form(held, plain, 1.0)
    y_inv = real_form(plain, held, 1.0)[:, mixed]
    z_inv = real_form(plain, plain, 1.0).T
    return [split_table(t) for t in (z_fwd, y_fwd, x_fwd, x_inv, y_inv, z_inv)]


def split(values):
    high = values.astype(jnp.bfloat16)
    return high, (values - high.astype(jnp.float32)).astype(jnp.bfloat16)


def dot(a, b):
    return jnp.dot(a, b, preferred_element_type=jnp.float32)


def times(values, table):
    high, low = split(values)
    return dot(high, table[0]) + (dot(low, table[0]) + dot(high, table[1]))


def apply(table, values):
    high, low = split(values)
    return dot(table[0], high) + (dot(table[0], low) + dot(table[1], high))


def plane(sent_ref, b, s):
    return jnp.concatenate([sent_ref[q * SIDE + b, s] for q in range(SIDE)], axis=0)


def forward_kernel(psi_ref, sent_ref, z_ref, y_ref, out_ref):
    for b in range(SIDE):
        first, second = plane(sent_ref, b, 0), plane(sent_ref, b, 1)
        rows = []
        for a in range(SIDE):
            psi = psi_ref[b * SIDE + a]
            rows.append(jnp.concatenate([psi * first, psi * second], axis=1))
        lines = times(jnp.concatenate(rows, axis=0), z_ref)
        cols = []
        for a in range(SIDE):
            part = lines[a * NG : (a + 1) * NG]
            cols.append(jnp.concatenate([part[:, :NG], part[:, NG:]], axis=0))
        spectrum = apply(y_ref, jnp.concatenate(cols, axis=1))
        for a in range(SIDE):
            out_ref[:, b * SIDE + a] = spectrum[:, a * NG : (a + 1) * NG].reshape(GROUP, 8, NG)


def middle_kernel(in_ref, kernel_ref, fwd_ref, inv_ref, out_ref):
    for ky in range(SIDE):
        cols = []
        for a in range(SIDE):
            at = a * 8 + ky
            cols.append(
                jnp.concatenate([in_ref[pl.ds(at, NG, stride=32), :], in_ref[pl.ds(at + 4, NG, stride=32), :]], axis=0)
            )
        spectrum = apply(fwd_ref, jnp.concatenate(cols, axis=1))
        weight = kernel_ref[ky]
        weight = jnp.concatenate([weight, weight], axis=0)
        weight = jnp.concatenate([weight] * SIDE, axis=1)
        back = apply(inv_ref, spectrum * weight)
        for a in range(SIDE):
            at = a * 8 + ky
            part = back[:, a * NG : (a + 1) * NG]
            out_ref[pl.ds(at, NG, stride=32), :] = part[:NG]
            out_ref[pl.ds(at + 4, NG, stride=32), :] = part[NG:]


def inverse_kernel(in_ref, sent_ref, y_ref, z_ref, out_ref):
    for b in range(SIDE):
        first, second = plane(sent_ref, b, 0), plane(sent_ref, b, 1)
        cols = [in_ref[:, b * SIDE + a].reshape(2 * NG, NG) for a in range(SIDE)]
        lines = apply(y_ref, jnp.concatenate(cols, axis=1))
        rows = []
        for a in range(SIDE):
            part = lines[:, a * NG : (a + 1) * NG]
            rows.append(jnp.concatenate([part[:NG], part[NG:]], axis=1))
        field = times(jnp.concatenate(rows, axis=0), z_ref)
        for a in range(SIDE):
            part = field[a * NG : (a + 1) * NG]
            out_ref[b * SIDE + a] = (first * part[:, :NG] + second * part[:, NG:]) * (-SCALE)


WORK = 2 * 2 * 3 * 2048 * 256 * 256


def call(kernel, shapes, *args):
    moved = sum(int(np.prod(a.shape)) * a.dtype.itemsize for a in args)
    moved += 4 * sum(int(np.prod(shape)) for shape in shapes)
    shapes = [jax.ShapeDtypeStruct(shape, jnp.float32) for shape in shapes]
    whole = pl.BlockSpec(memory_space=pltpu.VMEM)
    return pl.pallas_call(
        kernel,
        out_shape=shapes,
        in_specs=[whole] * len(args),
        out_specs=[whole] * len(shapes),
        compiler_params=pltpu.CompilerParams(vmem_limit_bytes=40 * 1024 * 1024),
        cost_estimate=pl.CostEstimate(flops=WORK, bytes_accessed=moved, transcendentals=0),
    )(*args)


def shift(values, axes, count, by):
    return lax.ppermute(values, axes, [(i, (i + by) % count) for i in range(count)])


def body(tables, orbitals, kernel, owners, picks):
    z_fwd, y_fwd, x_fwd, x_inv, y_inv, z_inv = [jnp.asarray(t) for t in tables]
    steps = owners.shape[0]
    y, zh, zl = lax.axis_index("y"), lax.axis_index("zh"), lax.axis_index("zl")

    psi = lax.all_to_all(orbitals.reshape(SIDE * SIDE, NG, NG), ("zh", "y"), 0, 0, tiled=True)

    def select(found, distance):
        return jnp.stack([lax.select_n(distance[s], *[f[s] for f in found]) for s in range(steps)])

    found = []
    for k in range(SIDE):
        at = (y + k) % SIDE
        part = [lax.dynamic_slice(orbitals, (picks[s, 0], at, 0, 0), (1, 1, NG, NG))[0, 0] for s in range(steps)]
        found.append(jnp.stack(part) if k == 0 else shift(jnp.stack(part), "y", SIDE, k))
    chosen = select(found, (y - owners // SIDE) % SIDE).reshape(steps, SIDE, 32, NG)
    found = []
    for k in range(SIDE):
        part = lax.dynamic_index_in_dim(chosen, (zl + k) % SIDE, 1, keepdims=False)
        found.append(part if k == 0 else shift(part, "zl", SIDE, k))
    sent = select(found, (zl - owners % SIDE) % SIDE)
    sent, psi = lax.optimization_barrier((sent, psi))
    sent = lax.all_to_all(jnp.broadcast_to(sent, (SIDE,) + sent.shape), "zh", 0, 0, tiled=True)
    sent = lax.all_to_all(jnp.broadcast_to(sent, (SIDE,) + sent.shape), "zl", 0, 0, tiled=True)
    sent = sent.reshape(16, steps, 32, NG)

    own = lax.dynamic_index_in_dim(kernel, y, 1, keepdims=False)
    own, psi, sent = lax.optimization_barrier((own, psi, sent))
    weight = lax.all_gather(own, "zh", axis=0, tiled=False)

    group = ("y", "x", "c")
    (spectrum,) = call(forward_kernel, [(GROUP, 16, 8, NG)], psi, sent, z_fwd, y_fwd)
    spectrum = lax.all_to_all(spectrum, group, 0, 0, tiled=True).reshape(GROUP * NG, NG)
    (spectrum,) = call(middle_kernel, [(GROUP * NG, NG)], spectrum, weight, x_fwd, x_inv)
    spectrum = lax.all_to_all(spectrum.reshape(GROUP, 16, 8, NG), group, 0, 0, tiled=True)
    (action,) = call(inverse_kernel, [(16, NG, NG)], spectrum, sent, y_inv, z_inv)
    action = lax.all_to_all(action, ("zh", "y"), 0, 0, tiled=True)
    return action.reshape(SIDE, SIDE, NG, NG)


def solution(mesh):
    fine = Mesh(np.asarray(mesh.devices).reshape(4, 4, 4, 4, 2), ("y", "zl", "zh", "x", "c"))
    band, fft = ("y", "zl"), ("zh", "x", "c")
    placed = (P(band, fft, None, None), P(None, fft, None), P(), P())
    return jax.shard_map(
        functools.partial(body, make_tables()),
        mesh=fine,
        in_specs=placed,
        out_specs=P(band, fft, None, None),
        check_vma=False,
    )
```
